32 devices in a mesh: parts: 2 (over x), req: 16 (over z, y, core).
Axes of the slice: x: 2, y: 2, z: 4, core: 2. Of those that a mesh axis runs over, the one named last changes fastest.
Arguments:
- conv_input: bfloat16 [32, 128, 8192], P(('parts', 'req')), parts along dimension 0, may hold values from -6 to 6
- gate_input: bfloat16 [32, 128, 8192], P(('parts', 'req')), parts along dimension 0, may hold values from -6 to 6
- step_size: bfloat16 [32, 128, 8192], P(('parts', 'req')), parts along dimension 0, may hold values from 7e-05 to 0.25
- state_maps: bfloat16 [32, 32, 128], P(('parts', 'req')), parts along dimension 0, may hold values from -12 to 12
- a_log: float32 [16, 8192], replicated, may hold values from 0 to 0.693
- conv_weight: bfloat16 [4, 8192], replicated, may hold values from -3 to 3
- conv_bias: float32 [8192], replicated, may hold values from -3 to 3
- skip_gain: float32 [8192], replicated, may hold values from 0.5 to 1.5
- owner_slot: int32 [32], P('parts'), parts along dimension 0, may hold values from 0 to 15, each once
- parent: int32 [32], P('parts'), parts along dimension 0, may hold values from 0 to 4, as said below
- lengths: int32 [32], P('parts'), parts along dimension 0, may hold values from 4 to 128, as said below
Outputs:
- scanned: bfloat16 [32, 128, 8192], P(('parts', 'req')), parts along dimension 0
The draws below stay inside these ranges and needn't reach their ends.
There are 2 independent parts, one for each index of `parts`. The reference program is written for one: setup_inputs(seed, part) draws one part's arguments, and reference() takes and returns one part's arrays. A program takes and returns all parts, laid end to end along the dimension named above; an argument that names none is the same for every part. Nothing has to cross between parts.
Inputs may be any that keep to these rules, and one draw needn't show every extreme that they name: owner_slot[n] is the index along req of the device that holds node n; each index appears once. parent[0] is 0 and means no parent; nodes 1 to 4 have parent 0; every other node has a parent among nodes 1 to 4. lengths[n] live tokens stand at the start of node n's positions, the rest are padding; some node fills all 128.
All inputs are finite; a program needn't handle non-finite values.
Results may differ from the reference program's by a relative error of at most 0.001.
Values sent between devices are 32-bit elements; how exact they have to be, the bound alone decides.
A program may use at most 128 MiB of HBM per device.

```python
import math
import jax
import jax.numpy as jnp
from jax import lax

STATE = 16
CONV = 4
INNER = 8192
NODE_TOKEN_SLOTS = 128
FEW = 4
TREE_NODE_COUNT = 16


def log_between(key, shape, low, high):
    return jnp.exp(jax.random.uniform(key, shape, jnp.float32, math.log(low), math.log(high)))


def draw_step_size(key, part):
    key = jax.random.fold_in(key, 11)
    random_key_list = jax.random.split(key, 6)
    fast_share = 0.5
    fast_mask = jax.random.bernoulli(random_key_list[0], fast_share, (INNER,))
    baseline_rate = jnp.where(fast_mask, log_between(random_key_list[1], (INNER,), 0.012, 0.03), log_between(random_key_list[2], (INNER,), 0.0003, 0.001))
    per_node_scale = log_between(random_key_list[3], (TREE_NODE_COUNT, 1, 1), 0.5, 2.0)
    coarse_scale = log_between(random_key_list[4], (TREE_NODE_COUNT, NODE_TOKEN_SLOTS, INNER), 0.5, 2.0)
    spike_mask = jax.random.bernoulli(random_key_list[5], 1.0 / 256.0, (TREE_NODE_COUNT, NODE_TOKEN_SLOTS, 1))
    value_entries = jnp.where(spike_mask, 0.25, baseline_rate[None, None, :] * per_node_scale * coarse_scale)
    return value_entries.astype(jnp.bfloat16)


def draw_parent(key, part):
    key = jax.random.fold_in(key, 23)
    node_ids = jnp.arange(TREE_NODE_COUNT, dtype=jnp.int32)
    chosen = jax.random.randint(key, (TREE_NODE_COUNT,), 1, FEW + 1, dtype=jnp.int32)
    linked = jnp.where(node_ids <= FEW, 0, chosen)
    return jnp.where(node_ids == TREE_NODE_COUNT - 1, FEW, linked).astype(jnp.int32)


def draw_lengths(key, part):
    key = jax.random.fold_in(key, 37)
    random_key_list = jax.random.split(key, 2)
    node_ids = jnp.arange(TREE_NODE_COUNT, dtype=jnp.int32)
    length_draw = jax.random.randint(random_key_list[0], (TREE_NODE_COUNT,), CONV, NODE_TOKEN_SLOTS + 1, dtype=jnp.int32)
    full_node = jax.random.randint(random_key_list[1], (), 0, TREE_NODE_COUNT, dtype=jnp.int32)
    return jnp.where(node_ids == full_node, NODE_TOKEN_SLOTS, length_draw).astype(jnp.int32)


def level_of(stream_key, dims, cuts, smallest, high):
    def one(dim, blocks):
        draws = jax.random.uniform(jax.random.fold_in(jax.random.fold_in(stream_key, 6), dim), (blocks,), jnp.float32, smallest / len(cuts), high / len(cuts))
        return jnp.repeat(jnp.exp(draws), dims[dim] // blocks).reshape((-1,) + (1,) * (len(dims) - dim - 1))

    factor_of = one(*cuts[0])
    for cut in cuts[1:]:
        factor_of = factor_of * one(*cut)
    return factor_of


def gaussian(stream_key, shape, deviation, limit, cuts=(), kind=jnp.bfloat16):
    factor_of = level_of(stream_key, shape, cuts, -0.22, 0.18) if cuts else 1.0
    values = jax.random.normal(stream_key, shape, jnp.float32) * deviation * factor_of
    return jnp.minimum(jnp.maximum(values, -limit), limit).astype(kind)


def setup_inputs(seed: int = 0, part: int = 0) -> dict:
    streams_of = jax.random.split(jax.random.key(seed), 12)
    part_splits = jax.random.split(jax.random.fold_in(streams_of[11], part), 12)
    conv_input = gaussian(part_splits[0], (TREE_NODE_COUNT, NODE_TOKEN_SLOTS, INNER), 1.0, 6.0, ((0, 16),))
    gate_input = gaussian(part_splits[1], (TREE_NODE_COUNT, NODE_TOKEN_SLOTS, INNER), 1.0, 6.0, ((0, 16),))
    step_size = draw_step_size(jax.random.fold_in(jax.random.fold_in(streams_of[11], part), 71), part)
    state_maps = gaussian(part_splits[3], (TREE_NODE_COUNT, 2 * STATE, NODE_TOKEN_SLOTS), 2.0, 12.0, ((0, 16),))
    a_log = jnp.clip(jax.random.uniform(streams_of[4], (STATE, INNER), jnp.float32, 0.0, 0.693), 0.0, 0.693)
    conv_weight = gaussian(streams_of[5], (CONV, INNER), CONV ** -0.5, 3.0)
    conv_bias = gaussian(streams_of[6], (INNER,), 0.5, 3.0, (), jnp.float32)
    skip_gain = jnp.clip(jax.random.uniform(streams_of[7], (INNER,), jnp.float32, 0.5, 1.5), 0.5, 1.5)
    owner_slot = jax.random.permutation(part_splits[8], TREE_NODE_COUNT).astype(jnp.int32)
    parent = draw_parent(jax.random.fold_in(jax.random.fold_in(streams_of[11], part), 71), part)
    lengths = draw_lengths(jax.random.fold_in(jax.random.fold_in(streams_of[11], part), 71), part)
    return dict(conv_input=conv_input, gate_input=gate_input, step_size=step_size, state_maps=state_maps, a_log=a_log, conv_weight=conv_weight, conv_bias=conv_bias, skip_gain=skip_gain, owner_slot=owner_slot, parent=parent, lengths=lengths)


def run_node(node_x, node_z, node_dt, node_maps, length, start_state, history, a_mat, conv_weight, conv_bias, skip_gain):
    slot_count = node_x.shape[0]
    tap_count = conv_weight.shape[0]
    states = a_mat.shape[0]
    extended = jnp.concatenate([history, node_x.astype(jnp.float32)], 0)
    pre_act = conv_bias[None, :]
    for k in range(tap_count):
        pre_act = pre_act + conv_weight[k].astype(jnp.float32)[None, :] * extended[k:k + slot_count]
    u_rows = jax.nn.silu(pre_act)
    live_mask = (jnp.arange(slot_count) < length).astype(jnp.float32)[:, None]
    dt_rows = node_dt.astype(jnp.float32) * live_mask
    b_rows = node_maps[:states].astype(jnp.float32).T
    c_rows = node_maps[states:].astype(jnp.float32).T

    def advance(carry_state, pieces):
        step_row, input_row, b_row, c_row = pieces
        carry_state = jnp.exp(a_mat * step_row[None, :]) * carry_state + b_row[:, None] * input_row[None, :]
        return carry_state, jnp.sum(c_row[:, None] * carry_state, 0)

    final_state, y_rows = lax.scan(advance, start_state, (dt_rows, dt_rows * u_rows, b_rows, c_rows))
    gate_act = jax.nn.silu(node_z.astype(jnp.float32))
    output = ((y_rows + skip_gain[None, :] * u_rows) * gate_act * live_mask).astype(jnp.bfloat16)
    tail_rows = lax.dynamic_slice_in_dim(extended, length, tap_count - 1, 0)
    return output, final_state, tail_rows


def reference(conv_input, gate_input, step_size, state_maps, a_log, conv_weight, conv_bias, skip_gain, owner_slot, parent, lengths):
    a_mat = -jnp.exp(a_log)

    def run_slot(node, start_state, history):
        slot = owner_slot[node]
        return run_node(conv_input[slot], gate_input[slot], step_size[slot], state_maps[slot], lengths[node], start_state, history, a_mat, conv_weight, conv_bias, skip_gain)

    zero_state = jnp.zeros((STATE, INNER), jnp.float32)
    zero_history = jnp.zeros((CONV - 1, INNER), jnp.float32)
    root_out, root_end, root_tail = run_slot(0, zero_state, zero_history)
    result = jnp.zeros((TREE_NODE_COUNT, NODE_TOKEN_SLOTS, INNER), jnp.bfloat16).at[owner_slot[0]].set(root_out)
    end_list = []
    tail_list = []
    for node in range(1, FEW + 1):
        block_out, block_end, block_tail = run_slot(node, root_end, root_tail)
        result = result.at[owner_slot[node]].set(block_out)
        end_list.append(block_end)
        tail_list.append(block_tail)
    few_ends = jnp.stack(end_list)
    few_tails = jnp.stack(tail_list)

    def question(node):
        above = parent[node] - 1
        question_out, _, _ = run_slot(node, few_ends[above], few_tails[above])
        return question_out

    question_ids = jnp.arange(FEW + 1, TREE_NODE_COUNT, dtype=jnp.int32)
    question_outs = lax.map(question, question_ids)
    result = result.at[owner_slot[question_ids]].set(question_outs)
    return result
```

```python
import functools
import math

import jax
import jax.numpy as jnp
from jax import lax
from jax.experimental import pallas as pl
from jax.experimental.pallas import tpu as pltpu
from jax.sharding import PartitionSpec as P

FEW = 4
TILE = 1024
PAD = 8
STEPS = 8
LOG2E = math.log2(math.e)
VMEM_LIMIT = 40 * 1024 * 1024


def silu(v):
    half = 0.5 * v
    return half + half * jnp.tanh(half)


def prepare(rows, len_, first, x_ref, dt_ref, w_ref, bias_ref, xs, us, dts, xds):
    slots = x_ref.shape[1]
    t_ids = lax.broadcasted_iota(jnp.int32, (slots, 128), 0)
    live = jnp.logical_and(t_ids >= first, t_ids < len_).astype(jnp.float32)
    for c in range(8):
        cols = pl.ds(c * 128, 128)
        base = c * rows
        xs[pl.ds(base + PAD, slots), :] = x_ref[0, :, cols].astype(jnp.float32)
        pre = bias_ref[0:1, cols]
        for k in range(w_ref.shape[0]):
            pre = pre + w_ref[k : k + 1, cols].astype(jnp.float32) * xs[
                pl.ds(base + PAD - w_ref.shape[0] + 1 + k, slots), :
            ]
        u = silu(pre)
        dt = dt_ref[0, :, cols].astype(jnp.float32) * live
        if us is not None:
            us[pl.ds(base, slots), :] = u
        dts[pl.ds(base, slots), :] = dt
        xds[pl.ds(base, slots), :] = dt * u


def tile_of(ref, rows, t):
    return ref[pl.ds(t, 8, stride=rows), :]


def state_kernel(
    groups, len_ref, maps_ref, x_ref, dt_ref, btile_ref, a_ref, w_ref, bias_ref, msg_ref, xs, dts, xds
):
    slots = x_ref.shape[1]
    rows = slots + PAD
    states = a_ref.shape[1]
    span = states // groups
    rim = w_ref.shape[0] - 1
    length = len_ref[0]
    prepare(rows, length, rim, x_ref, dt_ref, w_ref, bias_ref, xs, None, dts, xds)
    a = [a_ref[0, j] for j in range(states)]

    def steps(i, carry):
        h, total = list(carry[:-1]), carry[-1]
        for k in range(STEPS):
            t = i * STEPS + k
            dt = tile_of(dts, rows, t)
            xd = tile_of(xds, rows, t)
            for j in range(states):
                h[j] = jnp.exp2(a[j] * dt) * h[j] + maps_ref[t * 2 * states + j] * xd
            total = total + dt
        return (*h, total)

    zero = jnp.zeros((8, 128), jnp.float32)
    out = lax.fori_loop(0, slots // STEPS, steps, (zero,) * (states + 1))
    for g in range(groups):
        for j in range(span):
            msg_ref[g, j] = out[g * span + j]
        msg_ref[g, span] = out[states]
        for r in range(rim):
            msg_ref[g, span + 1 + r] = tile_of(xs, rows, PAD + r)
            msg_ref[g, span + 1 + 2 * rim + r] = tile_of(xs, rows, PAD + length - rim + r)
        msg_ref[g, span + 1 + 3 * rim] = btile_ref[g]
    for c in range(8):
        dts[pl.ds(c * rows, 8), :] = dt_ref[0, 0:8, pl.ds(c * 128, 128)].astype(jnp.float32)
    for g in range(groups):
        for r in range(rim):
            msg_ref[g, span + 1 + rim + r] = tile_of(dts, rows, r)


def exchange_kernel(
    groups, owner_ref, sel_ref, msg_ref, a_ref, w_ref, bias_ref, out_ref,
    recv, table, back, send1, recv1, send2, recv2, local_sem,
):
    n = msg_ref.shape[0]
    span = a_ref.shape[1] // groups
    taps = w_ref.shape[0]
    rim = taps - 1
    me = lax.axis_index("req")
    tile = me // groups
    first = (me % groups) * span

    barrier = pltpu.get_barrier_semaphore()

    def greet(k, c):
        pl.semaphore_signal(
            barrier, inc=1, device_id={"req": (me + k) % n}, device_id_type=pl.DeviceIdType.MESH
        )
        return c

    lax.fori_loop(1, n, greet, 0)
    pl.semaphore_wait(barrier, n - 1)

    def out_copy(k):
        to = (me + k) % n
        return pltpu.make_async_remote_copy(
            src_ref=msg_ref.at[to], dst_ref=recv.at[me],
            send_sem=send1.at[k], recv_sem=recv1.at[me],
            device_id={"req": to}, device_id_type=pl.DeviceIdType.MESH,
        )

    def in_copy(k):
        source = (me + k) % n
        return pltpu.make_async_remote_copy(
            src_ref=msg_ref.at[me], dst_ref=recv.at[source],
            send_sem=send1.at[k], recv_sem=recv1.at[source],
            device_id={"req": source}, device_id_type=pl.DeviceIdType.MESH,
        )

    lax.fori_loop(1, n, lambda k, c: (out_copy(k).start(), c)[1], 0)
    own = pltpu.make_async_copy(msg_ref.at[me], recv.at[me], local_sem)
    own.start()
    own.wait()
    lax.fori_loop(1, n, lambda k, c: (in_copy(k).wait_recv(), c)[1], 0)

    a = [a_ref[tile, first + j] for j in range(span)]
    w = [w_ref[k, tile] for k in range(taps)]
    bias = bias_ref[tile]
    zero = jnp.zeros((8, 128), jnp.float32)

    def node(k, start, history):
        slot = owner_ref[k]
        rows = list(history) + [recv[slot, span + 1 + r] for r in range(rim)]
        btile = recv[slot, span + 1 + 3 * rim]
        h = list(start)
        for r in range(rim):
            pre = bias
            for q in range(taps):
                pre = pre + w[q] * rows[r + q]
            dt = recv[slot, span + 1 + rim + r]
            xd = dt * silu(pre)
            for j in range(span):
                h[j] = jnp.exp2(a[j] * dt) * h[j] + btile[j : j + 1, r : r + 1] * xd
        total = recv[slot, span]
        h = [jnp.exp2(a[j] * total) * h[j] + recv[slot, j] for j in range(span)]
        tail = [recv[slot, span + 1 + 2 * rim + r] for r in range(rim)]
        return h, tail

    for r in range(span + rim):
        table[0, r] = zero
    root_end, root_tail = node(0, [zero] * span, [zero] * rim)
    for r, value in enumerate(root_end + root_tail):
        table[1, r] = value
    for k in range(1, FEW + 1):
        end, tail = node(k, root_end, root_tail)
        for r, value in enumerate(end + tail):
            table[1 + k, r] = value

    def back_out(k):
        to = (me + k) % n
        return pltpu.make_async_remote_copy(
            src_ref=back.at[to], dst_ref=out_ref.at[me],
            send_sem=send2.at[k], recv_sem=recv2.at[me],
            device_id={"req": to}, device_id_type=pl.DeviceIdType.MESH,
        )

    def back_in(k):
        source = (me + k) % n
        return pltpu.make_async_remote_copy(
            src_ref=back.at[me], dst_ref=out_ref.at[source],
            send_sem=send2.at[k], recv_sem=recv2.at[source],
            device_id={"req": source}, device_id_type=pl.DeviceIdType.MESH,
        )

    def fill(to):
        back[to] = table[sel_ref[to]]

    def reply(k, c):
        fill((me + k) % n)
        back_out(k).start()
        return c

    lax.fori_loop(1, n, reply, 0)
    fill(me)
    own = pltpu.make_async_copy(back.at[me], out_ref.at[me], local_sem)
    own.start()
    own.wait()

    def finish(k, c):
        out_copy(k).wait_send()
        back_out(k).wait_send()
        back_in(k).wait_recv()
        return c

    lax.fori_loop(1, n, finish, 0)


def scan_kernel(
    groups, len_ref, maps_ref, x_ref, dt_ref, z_ref, start_ref, a_ref, w_ref, bias_ref, skip_ref,
    out_ref, xs, us, dts, xds, ys
):
    slots = x_ref.shape[1]
    rows = slots + PAD
    states = a_ref.shape[1]
    span = states // groups
    rim = w_ref.shape[0] - 1
    length = len_ref[0]
    for r in range(rim):
        xs[pl.ds(PAD - rim + r, 8, stride=rows), :] = start_ref[0, span + r]
    prepare(rows, length, 0, x_ref, dt_ref, w_ref, bias_ref, xs, us, dts, xds)
    a = [a_ref[0, j] for j in range(states)]

    def steps(i, carry):
        h = list(carry)
        for k in range(STEPS):
            t = i * STEPS + k
            dt = tile_of(dts, rows, t)
            xd = tile_of(xds, rows, t)
            parts = []
            for j in range(states):
                h[j] = jnp.exp2(a[j] * dt) * h[j] + maps_ref[t * 2 * states + j] * xd
                part = maps_ref[t * 2 * states + states + j] * h[j]
                if j < 2:
                    parts.append(part)
                else:
                    parts[j % 2] = parts[j % 2] + part
            ys[pl.ds(t, 8, stride=rows), :] = parts[0] + parts[1]
        return tuple(h)

    start = tuple(start_ref[j // span, j % span] for j in range(states))
    lax.fori_loop(0, slots // STEPS, steps, start)
    t_ids = lax.broadcasted_iota(jnp.int32, (slots, 128), 0)
    live = (t_ids < length).astype(jnp.float32)
    for c in range(8):
        cols = pl.ds(c * 128, 128)
        rows_c = pl.ds(c * rows, slots)
        y = ys[rows_c, :] + skip_ref[0:1, cols] * us[rows_c, :]
        gate = silu(z_ref[0, :, cols].astype(jnp.float32)) * live
        out_ref[0, :, cols] = (y * gate).astype(jnp.bfloat16)


def body(
    conv_input, gate_input, step_size, state_maps, a_log, conv_weight, conv_bias, skip_gain,
    owner_slot, parent, lengths,
):
    n = owner_slot.shape[0]
    _, slots, inner = conv_input.shape
    states = a_log.shape[0]
    taps = conv_weight.shape[0]
    rim = taps - 1
    tiles = inner // TILE
    groups = n // tiles
    span = states // groups
    rows = slots + PAD
    message = span + 2 + 3 * rim

    me = lax.axis_index("req")
    ids = jnp.arange(n, dtype=jnp.int32)
    holds = owner_slot[None, :] == ids[:, None]
    my_len = jnp.sum(jnp.where(owner_slot == me, lengths, 0)).reshape(1)
    source = jnp.where(ids == 0, 0, jnp.where(ids <= FEW, 1, parent + 1))
    sel = jnp.sum(jnp.where(holds, source[None, :], 0), 1)

    maps = state_maps[0].astype(jnp.float32)
    flat_maps = maps.T.reshape(-1)
    btile = jnp.pad(maps[:states].reshape(groups, span, slots), ((0, 0), (0, 8 - span), (0, 0)))
    btile = btile[:, :, :128]
    a2 = (-LOG2E * jnp.exp(a_log)).reshape(states, tiles, 8, 128).transpose(1, 0, 2, 3)
    w_tiles = conv_weight.astype(jnp.float32).reshape(taps, tiles, 8, 128)
    bias_tiles = conv_bias.reshape(tiles, 8, 128)
    bias_row = conv_bias[None]
    skip_row = skip_gain[None]

    smem = pl.BlockSpec(memory_space=pltpu.SMEM)
    vmem = pl.BlockSpec(memory_space=pltpu.VMEM)
    big = pl.BlockSpec((1, slots, TILE), lambda b: (0, 0, b))
    a_spec = pl.BlockSpec((1, states, 8, 128), lambda b: (b, 0, 0, 0))
    w_spec = pl.BlockSpec((taps, TILE), lambda b: (0, b))
    row_spec = pl.BlockSpec((1, TILE), lambda b: (0, b))
    columns = pltpu.VMEM((8 * rows, 128), jnp.float32)

    msg = pl.pallas_call(
        functools.partial(state_kernel, groups),
        grid=(tiles,),
        out_shape=jax.ShapeDtypeStruct((n, message, 8, 128), jnp.float32),
        in_specs=[
            smem, smem, big, big,
            pl.BlockSpec((groups, 8, 128), lambda b: (0, 0, 0)),
            a_spec, w_spec, row_spec,
        ],
        out_specs=pl.BlockSpec((groups, message, 8, 128), lambda b: (b, 0, 0, 0)),
        scratch_shapes=[columns] * 3,
        compiler_params=pltpu.CompilerParams(vmem_limit_bytes=VMEM_LIMIT),
        name="state_pass",
    )(my_len, flat_maps, conv_input, step_size, btile, a2, conv_weight, bias_row)

    starts = pl.pallas_call(
        functools.partial(exchange_kernel, groups),
        out_shape=jax.ShapeDtypeStruct((n, span + rim, 8, 128), jnp.float32),
        in_specs=[smem, smem, vmem, vmem, vmem, vmem],
        out_specs=vmem,
        scratch_shapes=[
            pltpu.VMEM((n, message, 8, 128), jnp.float32),
            pltpu.VMEM((FEW + 2, span + rim, 8, 128), jnp.float32),
            pltpu.VMEM((n, span + rim, 8, 128), jnp.float32),
            pltpu.SemaphoreType.DMA((n,)),
            pltpu.SemaphoreType.DMA((n,)),
            pltpu.SemaphoreType.DMA((n,)),
            pltpu.SemaphoreType.DMA((n,)),
            pltpu.SemaphoreType.DMA,
        ],
        compiler_params=pltpu.CompilerParams(
            vmem_limit_bytes=VMEM_LIMIT, collective_id=0, has_side_effects=True
        ),
        name="exchange",
    )(owner_slot, sel, msg, a2, w_tiles, bias_tiles)

    return pl.pallas_call(
        functools.partial(scan_kernel, groups),
        grid=(tiles,),
        out_shape=jax.ShapeDtypeStruct((1, slots, inner), jnp.bfloat16),
        in_specs=[
            smem, smem, big, big, big,
            pl.BlockSpec((groups, span + rim, 8, 128), lambda b: (b, 0, 0, 0)),
            a_spec, w_spec, row_spec, row_spec,
        ],
        out_specs=big,
        scratch_shapes=[columns] * 5,
        compiler_params=pltpu.CompilerParams(vmem_limit_bytes=VMEM_LIMIT),
        name="full_scan",
    )(my_len, flat_maps, conv_input, step_size, gate_input, starts, a2, conv_weight, bias_row, skip_row)


def solution(mesh):
    blocks = P(("parts", "req"), None, None)
    return jax.shard_map(
        body,
        mesh=mesh,
        in_specs=(
            blocks, blocks, blocks, blocks,
            P(), P(), P(), P(),
            P("parts"), P("parts"), P("parts"),
        ),
        out_specs=blocks,
        check_vma=False,
    )
```

```python
import functools
import math

import jax
import jax.numpy as jnp
from jax import lax
from jax.experimental import pallas as pl
from jax.experimental.pallas import tpu as pltpu
from jax.sharding import PartitionSpec as P

FEW = 4
TILE = 1024
PAD = 8
STEPS = 8
LOG2E = math.log2(math.e)
VMEM_LIMIT = 40 * 1024 * 1024


def silu(v):
    half = 0.5 * v
    return half + half * jnp.tanh(half)


def column(b, c):
    return pl.ds(pl.multiple_of(b * TILE + c * 128, 128), 128)


def prepare(rows, b, length, first, x_ref, dt_ref, w_ref, bias_ref, xs, us, dts, xds):
    slots = x_ref.shape[1]
    taps = w_ref.shape[0]
    t_ids = lax.broadcasted_iota(jnp.int32, (slots, 128), 0)
    live = jnp.logical_and(t_ids >= first, t_ids < length).astype(jnp.float32)
    for c in range(8):
        cols = column(b, c)
        base = c * rows
        xs[pl.ds(base + PAD, slots), :] = x_ref[0, :, cols].astype(jnp.float32)
        pre = bias_ref[0:1, cols]
        for k in range(taps):
            pre = pre + w_ref[k : k + 1, cols] * xs[pl.ds(base + PAD - taps + 1 + k, slots), :]
        u = silu(pre)
        dt = dt_ref[0, :, cols].astype(jnp.float32) * live
        if us is not None:
            us[pl.ds(base, slots), :] = u
        dts[pl.ds(base, slots), :] = dt
        xds[pl.ds(base, slots), :] = dt * u


def tile_of(ref, rows, t):
    return ref[pl.ds(t, 8, stride=rows), :]


def tree_kernel(
    groups, len_ref, maps_ref, owner_ref, sel_ref, x_ref, dt_ref, z_ref, btile_ref, a_ref,
    w_ref, bias_ref, skip_ref, w_tiles, bias_tiles, out_ref,
    xs, us, dts, xds, ys, msg, recv, table, back, starts, send1, recv1, send2, recv2, local_sem,
):
    n = msg.shape[0]
    slots = x_ref.shape[1]
    rows = slots + PAD
    tiles, states = a_ref.shape[:2]
    span = states // groups
    taps = w_ref.shape[0]
    rim = taps - 1
    me = lax.axis_index("req")
    tile = me // groups
    first = (me % groups) * span
    length = len_ref[0]
    zero = jnp.zeros((8, 128), jnp.float32)

    barrier = pltpu.get_barrier_semaphore()

    def greet(k, c):
        pl.semaphore_signal(
            barrier, inc=1, device_id={"req": (me + k) % n}, device_id_type=pl.DeviceIdType.MESH
        )
        return c

    lax.fori_loop(1, n, greet, 0)
    pl.semaphore_wait(barrier, n - 1)

    def copy(src, dst, slot, sends, recvs, device):
        return pltpu.make_async_remote_copy(
            src_ref=src, dst_ref=dst, send_sem=sends.at[device], recv_sem=recvs.at[slot],
            device_id={"req": device}, device_id_type=pl.DeviceIdType.MESH,
        )

    def up_out(to):
        return copy(msg.at[to], recv.at[me], me, send1, recv1, to)

    def up_in(source):
        return copy(msg.at[source], recv.at[source], source, send1, recv1, source)

    def down_out(to):
        return copy(back.at[to], starts.at[me], me, send2, recv2, to)

    def down_in(source):
        return copy(back.at[source], starts.at[source], source, send2, recv2, source)

    for c in range(8):
        xs[pl.ds(c * rows, PAD), :] = zero

    def state_pass(r, unused):
        b = (tile + r) % tiles
        prepare(rows, b, length, rim, x_ref, dt_ref, w_ref, bias_ref, xs, None, dts, xds)
        a = [a_ref[b, j] for j in range(states)]

        def steps(i, carry):
            h, total = list(carry[:-1]), carry[-1]
            for k in range(STEPS):
                t = i * STEPS + k
                dt = tile_of(dts, rows, t)
                xd = tile_of(xds, rows, t)
                for j in range(states):
                    h[j] = jnp.exp2(a[j] * dt) * h[j] + maps_ref[t * 2 * states + j] * xd
                total = total + dt
            return (*h, total)

        out = lax.fori_loop(0, slots // STEPS, steps, (zero,) * (states + 1))
        for c in range(8):
            dts[pl.ds(c * rows, 8), :] = dt_ref[0, 0:8, column(b, c)].astype(jnp.float32)
        for g in range(groups):
            to = b * groups + g
            for j in range(span):
                msg[to, j] = out[g * span + j]
            msg[to, span] = out[states]
            for q in range(rim):
                msg[to, span + 1 + q] = tile_of(xs, rows, PAD + q)
                msg[to, span + 1 + rim + q] = tile_of(dts, rows, q)
                msg[to, span + 1 + 2 * rim + q] = tile_of(xs, rows, PAD + length - rim + q)
            msg[to, span + 1 + 3 * rim] = btile_ref[g]

            @pl.when(to != me)
            def _():
                up_out(to).start()

        return unused

    lax.fori_loop(0, tiles, state_pass, 0)
    own = pltpu.make_async_copy(msg.at[me], recv.at[me], local_sem)
    own.start()
    own.wait()
    lax.fori_loop(1, n, lambda k, c: (up_in((me + k) % n).wait_recv(), c)[1], 0)

    a = [a_ref[tile, first + j] for j in range(span)]
    w = [w_tiles[k, tile] for k in range(taps)]
    bias = bias_tiles[tile]

    def node(k, start, history):
        slot = owner_ref[k]
        x = list(history) + [recv[slot, span + 1 + q] for q in range(rim)]
        btile = recv[slot, span + 1 + 3 * rim]
        h = list(start)
        for q in range(rim):
            pre = bias
            for p in range(taps):
                pre = pre + w[p] * x[q + p]
            dt = recv[slot, span + 1 + rim + q]
            xd = dt * silu(pre)
            for j in range(span):
                h[j] = jnp.exp2(a[j] * dt) * h[j] + btile[j : j + 1, q : q + 1] * xd
        total = recv[slot, span]
        h = [jnp.exp2(a[j] * total) * h[j] + recv[slot, j] for j in range(span)]
        tail = [recv[slot, span + 1 + 2 * rim + q] for q in range(rim)]
        return h, tail

    for q in range(span + rim):
        table[0, q] = zero
    root_end, root_tail = node(0, [zero] * span, [zero] * rim)
    for q, value in enumerate(root_end + root_tail):
        table[1, q] = value
    for k in range(1, FEW + 1):
        end, tail = node(k, root_end, root_tail)
        for q, value in enumerate(end + tail):
            table[1 + k, q] = value

    def reply(k, c):
        to = ((tile + tiles - k // groups) % tiles) * groups + (me + k) % groups
        back[to] = table[sel_ref[to]]

        @pl.when(to != me)
        def _():
            down_out(to).start()

        return c

    lax.fori_loop(0, n, reply, 0)
    own = pltpu.make_async_copy(back.at[me], starts.at[me], local_sem)
    own.start()
    own.wait()

    def full_pass(r, unused):
        b = (tile + r) % tiles
        for g in range(groups):
            source = b * groups + g

            @pl.when(source != me)
            def _():
                down_in(source).wait_recv()

        for q in range(rim):
            xs[pl.ds(PAD - rim + q, 8, stride=rows), :] = starts[b * groups, span + q]
        prepare(rows, b, length, 0, x_ref, dt_ref, w_ref, bias_ref, xs, us, dts, xds)
        a = [a_ref[b, j] for j in range(states)]

        def steps(i, carry):
            h = list(carry)
            for k in range(STEPS):
                t = i * STEPS + k
                dt = tile_of(dts, rows, t)
                xd = tile_of(xds, rows, t)
                parts = []
                for j in range(states):
                    h[j] = jnp.exp2(a[j] * dt) * h[j] + maps_ref[t * 2 * states + j] * xd
                    part = maps_ref[t * 2 * states + states + j] * h[j]
                    if j < 2:
                        parts.append(part)
                    else:
                        parts[j % 2] = parts[j % 2] + part
                ys[pl.ds(t, 8, stride=rows), :] = parts[0] + parts[1]
            return tuple(h)

        start = tuple(starts[b * groups + j // span, j % span] for j in range(states))
        lax.fori_loop(0, slots // STEPS, steps, start)
        t_ids = lax.broadcasted_iota(jnp.int32, (slots, 128), 0)
        live = (t_ids < length).astype(jnp.float32)
        for c in range(8):
            cols = column(b, c)
            rows_c = pl.ds(c * rows, slots)
            y = ys[rows_c, :] + skip_ref[0:1, cols] * us[rows_c, :]
            gate = silu(z_ref[0, :, cols].astype(jnp.float32)) * live
            out_ref[0, :, cols] = (y * gate).astype(jnp.bfloat16)
        return unused

    lax.fori_loop(0, tiles, full_pass, 0)

    def finish(k, c):
        up_out((me + k) % n).wait_send()
        down_out((me + k) % n).wait_send()
        return c

    lax.fori_loop(1, n, finish, 0)


def body(
    conv_input, gate_input, step_size, state_maps, a_log, conv_weight, conv_bias, skip_gain,
    owner_slot, parent, lengths,
):
    n = owner_slot.shape[0]
    _, slots, inner = conv_input.shape
    states = a_log.shape[0]
    taps = conv_weight.shape[0]
    rim = taps - 1
    tiles = inner // TILE
    groups = n // tiles
    span = states // groups
    rows = slots + PAD
    message = span + 2 + 3 * rim

    me = lax.axis_index("req")
    ids = jnp.arange(n, dtype=jnp.int32)
    holds = owner_slot[None, :] == ids[:, None]
    my_len = jnp.sum(jnp.where(owner_slot == me, lengths, 0)).reshape(1)
    source = jnp.where(ids == 0, 0, jnp.where(ids <= FEW, 1, parent + 1))
    sel = jnp.sum(jnp.where(holds, source[None, :], 0), 1)

    maps = state_maps[0].astype(jnp.float32)
    flat_maps = maps.T.reshape(-1)
    btile = jnp.pad(maps[:states].reshape(groups, span, slots), ((0, 0), (0, 8 - span), (0, 0)))
    btile = btile[:, :, :128]
    a2 = (-LOG2E * jnp.exp(a_log)).reshape(states, tiles, 8, 128).transpose(1, 0, 2, 3)
    w_tiles = conv_weight.astype(jnp.float32).reshape(taps, tiles, 8, 128)
    bias_tiles = conv_bias.reshape(tiles, 8, 128)
    bias_row = conv_bias[None]
    skip_row = skip_gain[None]

    smem = pl.BlockSpec(memory_space=pltpu.SMEM)
    vmem = pl.BlockSpec(memory_space=pltpu.VMEM)
    columns = pltpu.VMEM((8 * rows, 128), jnp.float32)

    return pl.pallas_call(
        functools.partial(tree_kernel, groups),
        out_shape=jax.ShapeDtypeStruct((1, slots, inner), jnp.bfloat16),
        in_specs=[smem] * 4 + [vmem] * 10,
        out_specs=vmem,
        scratch_shapes=[columns] * 5
        + [
            pltpu.VMEM((n, message, 8, 128), jnp.float32),
            pltpu.VMEM((n, message, 8, 128), jnp.float32),
            pltpu.VMEM((FEW + 2, span + rim, 8, 128), jnp.float32),
            pltpu.VMEM((n, span + rim, 8, 128), jnp.float32),
            pltpu.VMEM((n, span + rim, 8, 128), jnp.float32),
        ]
        + [pltpu.SemaphoreType.DMA((n,))] * 4
        + [pltpu.SemaphoreType.DMA],
        compiler_params=pltpu.CompilerParams(
            vmem_limit_bytes=VMEM_LIMIT, collective_id=0, has_side_effects=True
        ),
        name="tree_scan",
    )(
        my_len, flat_maps, owner_slot, sel, conv_input, step_size, gate_input, btile, a2,
        conv_weight.astype(jnp.float32), bias_row, skip_row, w_tiles, bias_tiles,
    )


def solution(mesh):
    blocks = P(("parts", "req"), None, None)
    return jax.shard_map(
        body,
        mesh=mesh,
        in_specs=(
            blocks, blocks, blocks, blocks,
            P(), P(), P(), P(),
            P("parts"), P("parts"), P("parts"),
        ),
        out_specs=blocks,
        check_vma=False,
    )
```

```python
import functools
import math

import jax
import jax.numpy as jnp
from jax import lax
from jax.experimental import pallas as pl
from jax.experimental.pallas import tpu as pltpu
from jax.sharding import PartitionSpec as P

FEW = 4
TILE = 1024
PAD = 8
STEPS = 16
LOG2E = math.log2(math.e)
VMEM_LIMIT = 40 * 1024 * 1024


def silu(v):
    half = 0.5 * v
    return half + half * jnp.tanh(half)


def column(b, c):
    return pl.ds(pl.multiple_of(b * TILE + c * 128, 128), 128)


def tree_kernel(
    groups, len_ref, owner_ref, above_ref, sel_ref, x_ref, dt_ref, z_ref, tail_ref, maps_ref, a_ref,
    w_ref, bias_ref, skip_ref, w_tiles, bias_tiles, out_ref,
    xs, us, dts, xds, ys, heads, tails, picked, history, msg, recv, table, back, starts,
    send_a, recv_a, send_b, recv_b, send1, recv1, send2, recv2, local_sem,
):
    n = msg.shape[0]
    slots = x_ref.shape[1]
    rows = slots + PAD
    tiles, states = a_ref.shape[:2]
    span = states // groups
    taps = w_ref.shape[0]
    rim = taps - 1
    me = lax.axis_index("req")
    tile = me // groups
    lead = me % groups == 0
    first = (me % groups) * span
    length = len_ref[0]
    zero = jnp.zeros((8, 128), jnp.float32)

    barrier = pltpu.get_barrier_semaphore()

    def greet(k, c):
        pl.semaphore_signal(
            barrier, inc=1, device_id={"req": (me + k) % n}, device_id_type=pl.DeviceIdType.MESH
        )
        return c

    lax.fori_loop(1, n, greet, 0)
    pl.semaphore_wait(barrier, n - 1)

    def copy(src, dst, slot, sends, recvs, sent, device):
        return pltpu.make_async_remote_copy(
            src_ref=src, dst_ref=dst, send_sem=sends.at[sent], recv_sem=recvs.at[slot],
            device_id={"req": device}, device_id_type=pl.DeviceIdType.MESH,
        )

    def own(src, dst):
        mine = pltpu.make_async_copy(src, dst, local_sem)
        mine.start()
        mine.wait()

    def tail_out(b):
        return copy(tail_ref.at[b], tails.at[me], me, send_a, recv_a, b, b * groups)

    def tail_in(source):
        return copy(tail_ref.at[0], tails.at[source], source, send_a, recv_a, 0, source)

    def past_out(to):
        return copy(picked.at[to], history.at[tile], tile, send_b, recv_b, to, to)

    def past_in(b):
        return copy(picked.at[0], history.at[b], b, send_b, recv_b, 0, b * groups)

    def up_out(to):
        return copy(msg.at[to], recv.at[me], me, send1, recv1, to, to)

    def up_in(source):
        return copy(msg.at[source], recv.at[source], source, send1, recv1, source, source)

    def down_out(to):
        return copy(back.at[to], starts.at[me], me, send2, recv2, to, to)

    def down_in(source):
        return copy(back.at[source], starts.at[source], source, send2, recv2, source, source)

    def away(device, action):
        @pl.when(device != me)
        def _():
            action()

    def send_tail(r, c):
        b = (tile + r) % tiles
        away(b * groups, lambda: tail_out(b).start())
        return c

    lax.fori_loop(0, tiles, send_tail, 0)
    for c in range(8):
        xs[pl.ds(c * rows, PAD), :] = zero
    t_ids = lax.broadcasted_iota(jnp.int32, (slots, 128), 0)
    live = (t_ids < length).astype(jnp.float32)

    def column(b, c):
        return pl.ds(pl.multiple_of(b * TILE + c * 128, 128), 128)

    def base(b, c):
        return pl.multiple_of((b * 8 + c) * rows, 8)

    def tile_rows(b, t):
        return pl.ds(b * 8 * rows + t, 8, stride=rows)

    def prepare(b, carry):
        for c in range(8):
            cols = column(b, c)
            to = pl.ds(base(b, c), slots)
            xs[pl.ds(c * rows + PAD, slots), :] = x_ref[0, :, cols].astype(jnp.float32)
            pre = bias_ref[0:1, cols]
            for k in range(taps):
                pre = pre + w_ref[k : k + 1, cols] * xs[
                    pl.ds(c * rows + PAD - rim + k, slots), :
                ]
            u = silu(pre)
            dt = dt_ref[0, :, cols].astype(jnp.float32) * live
            us[to, :] = u
            dts[to, :] = dt
            xds[to, :] = dt * u
        for q in range(rim):
            heads[b, q] = xs[pl.ds(PAD + q, 8, stride=rows), :]
        return carry

    lax.fori_loop(0, tiles // 2, prepare, 0)

    @pl.when(lead)
    def _():
        own(tail_ref.at[tile], tails.at[me])
        lax.fori_loop(1, n, lambda k, c: (tail_in((me + k) % n).wait_recv(), c)[1], 0)

        def pick(k, c):
            to = ((tile + tiles - k // groups) % tiles) * groups + k % groups
            known = (sel_ref[to] > 0).astype(jnp.float32)
            for q in range(rim):
                picked[to, q] = tails[above_ref[to], q] * known
            away(to, lambda: past_out(to).start())
            return c

        lax.fori_loop(0, n, pick, 0)
        own(picked.at[me], history.at[tile])

    lax.fori_loop(tiles // 2, tiles, prepare, 0)

    def correct(b, carry):
        away(b * groups, lambda: past_in(b).wait_recv())
        x = [history[b, q] for q in range(rim)] + [heads[b, q] for q in range(rim)]
        for q in range(rim):
            pre = bias_tiles[b]
            for k in range(taps):
                pre = pre + w_tiles[k, b] * x[q + k]
            u = silu(pre)
            us[tile_rows(b, q), :] = u
            xds[tile_rows(b, q), :] = dts[tile_rows(b, q), :] * u
        return carry

    lax.fori_loop(0, tiles, correct, 0)

    def state_pass(r, unused):
        b = (tile + r) % tiles
        a = [a_ref[b, j] for j in range(states)]

        def steps(i, carry):
            h, total = list(carry[:-1]), carry[-1]
            for k in range(STEPS):
                t = i * STEPS + k
                dt = dts[tile_rows(b, t), :]
                xd = xds[tile_rows(b, t), :]
                for j in range(states):
                    into = maps_ref[pl.ds(t * 2 * states + j, 1), :]
                    h[j] = jnp.exp2(a[j] * dt) * h[j] + into * xd
                total = total + dt
            return (*h, total)

        out = lax.fori_loop(0, slots // STEPS, steps, (zero,) * (states + 1))
        for g in range(groups):
            to = b * groups + g
            for j in range(span):
                msg[to, j] = out[g * span + j]
            msg[to, span] = out[states]
            away(to, lambda: up_out(to).start())
        return unused

    lax.fori_loop(0, tiles, state_pass, 0)
    own(msg.at[me], recv.at[me])
    lax.fori_loop(1, n, lambda k, c: (up_in((me + k) % n).wait_recv(), c)[1], 0)

    for j in range(span):
        a = a_ref[tile, first + j]
        root = recv[owner_ref[0], j]
        table[0, j] = zero
        table[1, j] = root
        for k in range(1, FEW + 1):
            slot = owner_ref[k]
            table[1 + k, j] = jnp.exp2(a * recv[slot, span]) * root + recv[slot, j]

    def reply(k, c):
        to = ((tile + tiles - k // groups) % tiles) * groups + (me + k) % groups
        back[to] = table[sel_ref[to]]
        away(to, lambda: down_out(to).start())
        return c

    lax.fori_loop(0, n, reply, 0)
    own(back.at[me], starts.at[me])

    def full_pass(r, unused):
        b = (tile + r) % tiles
        for g in range(groups):
            source = b * groups + g
            away(source, lambda: down_in(source).wait_recv())
        a = [a_ref[b, j] for j in range(states)]

        def steps(i, carry):
            h = list(carry)
            for k in range(STEPS):
                t = i * STEPS + k
                dt = dts[tile_rows(b, t), :]
                xd = xds[tile_rows(b, t), :]
                parts = []
                for j in range(states):
                    into = maps_ref[pl.ds(t * 2 * states + j, 1), :]
                    h[j] = jnp.exp2(a[j] * dt) * h[j] + into * xd
                    part = maps_ref[pl.ds(t * 2 * states + states + j, 1), :] * h[j]
                    if j < 2:
                        parts.append(part)
                    else:
                        parts[j % 2] = parts[j % 2] + part
                ys[pl.ds(t, 8, stride=rows), :] = parts[0] + parts[1]
            return tuple(h)

        start = tuple(starts[b * groups + j // span, j % span] for j in range(states))
        lax.fori_loop(0, slots // STEPS, steps, start)
        for c in range(8):
            cols = column(b, c)
            y = ys[pl.ds(c * rows, slots), :] + skip_ref[0:1, cols] * us[pl.ds(base(b, c), slots), :]
            gate = silu(z_ref[0, :, cols].astype(jnp.float32)) * live
            out_ref[0, :, cols] = (y * gate).astype(jnp.bfloat16)
        return unused

    lax.fori_loop(0, tiles, full_pass, 0)

    def finish(k, c):
        to = (me + k) % n
        up_out(to).wait_send()
        down_out(to).wait_send()

        @pl.when(lead)
        def _():
            past_out(to).wait_send()

        return c

    lax.fori_loop(1, n, finish, 0)
    lax.fori_loop(
        0, tiles, lambda b, c: (away(b * groups, lambda: tail_out(b).wait_send()), c)[1], 0
    )


def body(
    conv_input, gate_input, step_size, state_maps, a_log, conv_weight, conv_bias, skip_gain,
    owner_slot, parent, lengths,
):
    n = owner_slot.shape[0]
    _, slots, inner = conv_input.shape
    states = a_log.shape[0]
    taps = conv_weight.shape[0]
    rim = taps - 1
    tiles = inner // TILE
    groups = n // tiles
    span = states // groups
    rows = slots + PAD

    me = lax.axis_index("req")
    ids = jnp.arange(n, dtype=jnp.int32)
    holds = owner_slot[None, :] == ids[:, None]
    my_len = jnp.sum(jnp.where(owner_slot == me, lengths, 0))
    source = jnp.where(ids == 0, 0, jnp.where(ids <= FEW, 1, parent + 1))
    sel = jnp.sum(jnp.where(holds, source[None, :], 0), 1)
    above = jnp.sum(jnp.where(ids[None, :] == jnp.maximum(sel - 1, 0)[:, None], owner_slot, 0), 1)

    maps = jnp.broadcast_to(
        state_maps[0].astype(jnp.float32).T.reshape(-1, 1), (slots * 2 * states, 128)
    )
    tail = lax.dynamic_slice_in_dim(conv_input[0], my_len - rim, rim, 0).astype(jnp.float32)
    tail = tail.reshape(rim, tiles, 8, 128).transpose(1, 0, 2, 3)
    a2 = (-LOG2E * jnp.exp(a_log)).reshape(states, tiles, 8, 128).transpose(1, 0, 2, 3)
    weight = conv_weight.astype(jnp.float32)
    w_tiles = weight.reshape(taps, tiles, 8, 128)
    bias_tiles = conv_bias.reshape(tiles, 8, 128)

    smem = pl.BlockSpec(memory_space=pltpu.SMEM)
    vmem = pl.BlockSpec(memory_space=pltpu.VMEM)
    one = pltpu.VMEM((8 * rows, 128), jnp.float32)
    every = pltpu.VMEM((tiles * 8 * rows, 128), jnp.float32)

    def boxes(*lead):
        return pltpu.VMEM((*lead, 8, 128), jnp.float32)

    return pl.pallas_call(
        functools.partial(tree_kernel, groups),
        out_shape=jax.ShapeDtypeStruct((1, slots, inner), jnp.bfloat16),
        in_specs=[smem] * 4 + [vmem] * 11,
        out_specs=vmem,
        scratch_shapes=[one, every, every, every, one]
        + [boxes(tiles, rim), boxes(n, rim), boxes(n, rim), boxes(tiles, rim)]
        + [boxes(n, span + 1), boxes(n, span + 1), boxes(FEW + 2, span)]
        + [boxes(n, span), boxes(n, span)]
        + [pltpu.SemaphoreType.DMA((count,)) for count in (tiles, n, n, tiles, n, n, n, n)]
        + [pltpu.SemaphoreType.DMA],
        compiler_params=pltpu.CompilerParams(
            vmem_limit_bytes=VMEM_LIMIT, collective_id=0, has_side_effects=True
        ),
        name="tree_scan",
    )(
        my_len.reshape(1), owner_slot, above, sel, conv_input, step_size, gate_input, tail, maps,
        a2, weight, conv_bias[None], skip_gain[None], w_tiles, bias_tiles,
    )


def solution(mesh):
    blocks = P(("parts", "req"), None, None)
    return jax.shard_map(
        body,
        mesh=mesh,
        in_specs=(
            blocks, blocks, blocks, blocks,
            P(), P(), P(), P(),
            P("parts"), P("parts"), P("parts"),
        ),
        out_specs=blocks,
        check_vma=False,
    )
```

```python
import functools
import math

import jax
import jax.numpy as jnp
from jax import lax
from jax.experimental import pallas as pl
from jax.experimental.pallas import tpu as pltpu
from jax.sharding import PartitionSpec as P

FEW = 4
TILE = 1024
PAD = 8
STEPS = 16
LOG2E = math.log2(math.e)
VMEM_LIMIT = 40 * 1024 * 1024


def silu(v):
    half = 0.5 * v
    return half + half * jnp.tanh(half)


def column(b, c):
    return pl.ds(pl.multiple_of(b * TILE + c * 128, 128), 128)


def relate_kernel(len_ref, owner_ref, parent_ref, mine_ref, above_ref, sel_ref):
    n = owner_ref.shape[0]
    me = lax.axis_index("req")
    length = 0
    for k in range(n):
        length = length + jnp.where(owner_ref[k] == me, len_ref[k], 0)
    mine_ref[0] = length

    def relate(k, c):
        kind = jnp.where(k == 0, 0, jnp.where(k <= FEW, 1, parent_ref[k] + 1))
        to = owner_ref[k]
        sel_ref[to] = kind
        above_ref[to] = owner_ref[jnp.maximum(kind - 1, 0)]
        return c

    lax.fori_loop(0, n, relate, 0)


def tree_kernel(
    groups, len_ref, owner_ref, above_ref, sel_ref, x_ref, dt_ref, z_ref, tail_ref, maps_ref, alog_ref,
    w_ref, bias_ref, skip_ref, out_ref,
    xs, us, dts, xds, gates, ys, acols, a_ref, w_tiles, heads, tails, picked, history, msg, recv, table, back, starts,
    send_a, recv_a, send_b, recv_b, send1, recv1, send2, recv2, local_sem,
):
    n = msg.shape[0]
    slots = x_ref.shape[1]
    rows = slots + PAD
    tiles, states = a_ref.shape[:2]
    span = states // groups
    taps = w_ref.shape[0]
    rim = taps - 1
    me = lax.axis_index("req")
    tile = me // groups
    lead = me % groups == 0
    first = (me % groups) * span
    length = len_ref[0]
    zero = jnp.zeros((8, 128), jnp.float32)

    barrier = pltpu.get_barrier_semaphore()

    def greet(k, c):
        pl.semaphore_signal(
            barrier, inc=1, device_id={"req": (me + k) % n}, device_id_type=pl.DeviceIdType.MESH
        )
        return c

    lax.fori_loop(1, n, greet, 0)
    pl.semaphore_wait(barrier, n - 1)

    def copy(src, dst, slot, sends, recvs, sent, device):
        return pltpu.make_async_remote_copy(
            src_ref=src, dst_ref=dst, send_sem=sends.at[sent], recv_sem=recvs.at[slot],
            device_id={"req": device}, device_id_type=pl.DeviceIdType.MESH,
        )

    def own(src, dst):
        mine = pltpu.make_async_copy(src, dst, local_sem)
        mine.start()
        mine.wait()

    def tail_out(b):
        return copy(tail_ref.at[b], tails.at[me], me, send_a, recv_a, b, b * groups)

    def tail_in(source):
        return copy(tail_ref.at[0], tails.at[source], source, send_a, recv_a, 0, source)

    def past_out(to):
        return copy(picked.at[to], history.at[tile], tile, send_b, recv_b, to, to)

    def past_in(b):
        return copy(picked.at[0], history.at[b], b, send_b, recv_b, 0, b * groups)

    def up_out(to):
        return copy(msg.at[to], recv.at[me], me, send1, recv1, to, to)

    def up_in(source):
        return copy(msg.at[source], recv.at[source], source, send1, recv1, source, source)

    def down_out(to):
        return copy(back.at[to], starts.at[me], me, send2, recv2, to, to)

    def down_in(source):
        return copy(back.at[source], starts.at[source], source, send2, recv2, source, source)

    def away(device, action):
        @pl.when(device != me)
        def _():
            action()

    def column(b, c):
        return pl.ds(pl.multiple_of(b * TILE + c * 128, 128), 128)

    def send_tail(r, cc):
        b = (tile + r) % tiles
        away(b * groups, lambda: tail_out(b).start())
        return cc

    lax.fori_loop(0, tiles, send_tail, 0)
    for c in range(8):
        xs[pl.ds(c * rows, PAD), :] = zero
    t_ids = lax.broadcasted_iota(jnp.int32, (slots, 128), 0)
    live = (t_ids < length).astype(jnp.float32)

    def base(b, c):
        return pl.multiple_of((b * 8 + c) * rows, 8)

    def tile_rows(b, t):
        return pl.ds(b * 8 * rows + t, 8, stride=rows)

    def prepare(b, carry):
        for c in range(8):
            cols = column(b, c)
            to = pl.ds(base(b, c), slots)
            xs[pl.ds(c * rows + PAD, slots), :] = x_ref[0, :, cols].astype(jnp.float32)
            pre = bias_ref[0:1, cols]
            for k in range(taps):
                pre = pre + w_ref[k : k + 1, cols] * xs[
                    pl.ds(c * rows + PAD - rim + k, slots), :
                ]
            u = silu(pre)
            dt = dt_ref[0, :, cols].astype(jnp.float32) * live
            us[to, :] = u
            dts[to, :] = dt
            xds[to, :] = dt * u
            acols[pl.ds(c * 24, states), :] = -LOG2E * jnp.exp(alog_ref[:, cols])
            for k in range(taps):
                w_tiles[b, k, c : c + 1, :] = w_ref[k : k + 1, cols]
            w_tiles[b, taps, c : c + 1, :] = bias_ref[0:1, cols]
        for j in range(states):
            a_ref[b, j] = acols[pl.ds(j, 8, stride=24), :]
        for q in range(rim):
            heads[b, q] = xs[pl.ds(PAD + q, 8, stride=rows), :]
        return carry

    lax.fori_loop(0, tiles // 2, prepare, 0)

    @pl.when(lead)
    def _():
        own(tail_ref.at[tile], tails.at[me])
        lax.fori_loop(1, n, lambda k, c: (tail_in((me + k) % n).wait_recv(), c)[1], 0)

        def pick(k, c):
            to = ((tile + tiles - k // groups) % tiles) * groups + k % groups
            known = (sel_ref[to] > 0).astype(jnp.float32)
            for q in range(rim):
                picked[to, q] = tails[above_ref[to], q] * known
            away(to, lambda: past_out(to).start())
            return c

        lax.fori_loop(0, n, pick, 0)
        own(picked.at[me], history.at[tile])

    lax.fori_loop(tiles // 2, tiles, prepare, 0)

    def correct(b, carry):
        away(b * groups, lambda: past_in(b).wait_recv())
        x = [history[b, q] for q in range(rim)] + [heads[b, q] for q in range(rim)]
        for q in range(rim):
            pre = w_tiles[b, taps]
            for k in range(taps):
                pre = pre + w_tiles[b, k] * x[q + k]
            u = silu(pre)
            us[tile_rows(b, q), :] = u
            xds[tile_rows(b, q), :] = dts[tile_rows(b, q), :] * u
        return carry

    lax.fori_loop(0, tiles, correct, 0)

    def state_pass(r, unused):
        b = (tile + r) % tiles
        a = [a_ref[b, j] for j in range(states)]

        def steps(i, carry):
            h, total = list(carry[:-1]), carry[-1]
            for k in range(STEPS):
                t = i * STEPS + k
                dt = dts[tile_rows(b, t), :]
                xd = xds[tile_rows(b, t), :]
                for j in range(states):
                    into = maps_ref[pl.ds(t * 2 * states + j, 1), :]
                    h[j] = jnp.exp2(a[j] * dt) * h[j] + into * xd
                total = total + dt
            return (*h, total)

        out = lax.fori_loop(0, slots // STEPS, steps, (zero,) * (states + 1))
        for g in range(groups):
            to = b * groups + g
            for j in range(span):
                msg[to, j] = out[g * span + j]
            msg[to, span] = out[states]
            away(to, lambda: up_out(to).start())
        return unused

    lax.fori_loop(0, tiles, state_pass, 0)

    def gate(b, carry):
        for c in range(8):
            cols = column(b, c)
            at = pl.ds(base(b, c), slots)
            value = silu(z_ref[0, :, cols].astype(jnp.float32)) * live
            gates[at, :] = value
            us[at, :] = skip_ref[0:1, cols] * us[at, :] * value
        return carry

    lax.fori_loop(0, tiles, gate, 0)
    own(msg.at[me], recv.at[me])
    lax.fori_loop(1, n, lambda k, c: (up_in((me + k) % n).wait_recv(), c)[1], 0)

    for j in range(span):
        a = a_ref[tile, first + j]
        root = recv[owner_ref[0], j]
        table[0, j] = zero
        table[1, j] = root
        for k in range(1, FEW + 1):
            slot = owner_ref[k]
            table[1 + k, j] = jnp.exp2(a * recv[slot, span]) * root + recv[slot, j]

    def reply(k, c):
        to = ((tile + tiles - k // groups) % tiles) * groups + (me + k) % groups
        back[to] = table[sel_ref[to]]
        away(to, lambda: down_out(to).start())
        return c

    lax.fori_loop(0, n, reply, 0)
    own(back.at[me], starts.at[me])

    def full_pass(r, unused):
        b = (tile + r) % tiles
        for g in range(groups):
            source = b * groups + g
            away(source, lambda: down_in(source).wait_recv())
        a = [a_ref[b, j] for j in range(states)]

        def steps(i, carry):
            h = list(carry)
            for k in range(STEPS):
                t = i * STEPS + k
                dt = dts[tile_rows(b, t), :]
                xd = xds[tile_rows(b, t), :]
                parts = []
                for j in range(states):
                    into = maps_ref[pl.ds(t * 2 * states + j, 1), :]
                    h[j] = jnp.exp2(a[j] * dt) * h[j] + into * xd
                    part = maps_ref[pl.ds(t * 2 * states + states + j, 1), :] * h[j]
                    if j < 2:
                        parts.append(part)
                    else:
                        parts[j % 2] = parts[j % 2] + part
                ys[pl.ds(t, 8, stride=rows), :] = parts[0] + parts[1]
            return tuple(h)

        start = tuple(starts[b * groups + j // span, j % span] for j in range(states))
        lax.fori_loop(0, slots // STEPS, steps, start)
        for c in range(8):
            cols = column(b, c)
            at = pl.ds(base(b, c), slots)
            y = ys[pl.ds(c * rows, slots), :] * gates[at, :] + us[at, :]
            out_ref[0, :, cols] = y.astype(jnp.bfloat16)
        return unused

    lax.fori_loop(0, tiles, full_pass, 0)

    def finish(k, c):
        to = (me + k) % n
        up_out(to).wait_send()
        down_out(to).wait_send()

        @pl.when(lead)
        def _():
            past_out(to).wait_send()

        return c

    lax.fori_loop(1, n, finish, 0)
    lax.fori_loop(
        0, tiles, lambda b, c: (away(b * groups, lambda: tail_out(b).wait_send()), c)[1], 0
    )


def body(
    conv_input, gate_input, step_size, state_maps, a_log, conv_weight, conv_bias, skip_gain,
    owner_slot, parent, lengths,
):
    n = owner_slot.shape[0]
    _, slots, inner = conv_input.shape
    states = a_log.shape[0]
    taps = conv_weight.shape[0]
    rim = taps - 1
    tiles = inner // TILE
    groups = n // tiles
    span = states // groups
    rows = slots + PAD

    maps = jnp.broadcast_to(
        state_maps[0].astype(jnp.float32).T.reshape(-1, 1), (slots * 2 * states, 128)
    )
    smem = pl.BlockSpec(memory_space=pltpu.SMEM)
    vmem = pl.BlockSpec(memory_space=pltpu.VMEM)
    my_len, above, sel = pl.pallas_call(
        relate_kernel,
        out_shape=[jax.ShapeDtypeStruct((count,), jnp.int32) for count in (1, n, n)],
        in_specs=[smem] * 3,
        out_specs=[smem] * 3,
        name="relate",
    )(lengths, owner_slot, parent)
    tail = lax.dynamic_slice_in_dim(conv_input[0], my_len[0] - rim, rim, 0).astype(jnp.float32)
    tail = tail.reshape(rim, tiles, 8, 128).transpose(1, 0, 2, 3)
    one = pltpu.VMEM((8 * rows, 128), jnp.float32)
    every = pltpu.VMEM((tiles * 8 * rows, 128), jnp.float32)

    def boxes(*lead):
        return pltpu.VMEM((*lead, 8, 128), jnp.float32)

    return pl.pallas_call(
        functools.partial(tree_kernel, groups),
        out_shape=jax.ShapeDtypeStruct((1, slots, inner), jnp.bfloat16),
        in_specs=[smem] * 4 + [vmem] * 9,
        out_specs=vmem,
        scratch_shapes=[one, every, every, every, every, one]
        + [pltpu.VMEM((8 * 24, 128), jnp.float32)]
        + [boxes(tiles, states), boxes(tiles, taps + 1)]
        + [boxes(tiles, rim), boxes(n, rim), boxes(n, rim), boxes(tiles, rim)]
        + [boxes(n, span + 1), boxes(n, span + 1), boxes(FEW + 2, span)]
        + [boxes(n, span), boxes(n, span)]
        + [pltpu.SemaphoreType.DMA((count,)) for count in (tiles, n, n, tiles, n, n, n, n)]
        + [pltpu.SemaphoreType.DMA],
        compiler_params=pltpu.CompilerParams(
            vmem_limit_bytes=VMEM_LIMIT, collective_id=0, has_side_effects=True
        ),
        name="tree_scan",
    )(
        my_len, owner_slot, above, sel, conv_input, step_size, gate_input, tail, maps,
        a_log, conv_weight.astype(jnp.float32), conv_bias[None], skip_gain[None],
    )


def solution(mesh):
    blocks = P(("parts", "req"), None, None)
    return jax.shard_map(
        body,
        mesh=mesh,
        in_specs=(
            blocks, blocks, blocks, blocks,
            P(), P(), P(), P(),
            P("parts"), P("parts"), P("parts"),
        ),
        out_specs=blocks,
        check_vma=False,
    )
```
